256 devices in a mesh: band: 4 (over y), ga: 64 (over x, z, core).
Axes of the slice: x: 4, y: 4, z: 8, core: 2. Of those that a mesh axis runs over, the one named last changes fastest.
Arguments:
- psi: bfloat16 [1024, 2, 90112], P('band', None, 'ga'), may hold values from -48 to 48
- potential: float32 [128, 128, 128], P('ga'), may hold values from -5 to 5
- gmap: int32 [90112], P('ga'), may hold values from 0 to 4095, as said below
- colxy: int32 [2048], replicated, may hold values from 0 to 16383, as said below
Outputs:
- new_psi: bfloat16 [1024, 2, 90112], P('band', None, 'ga')
The draws below stay inside these ranges and needn't reach their ends.
Inputs may be any that keep to these rules, and one draw needn't show every extreme that they name: `gmap`: each block of 1408 entries of one index of ga lists that device's columns in order; the z frequencies of one column form one contiguous cyclic range that holds zero, from its lowest to its highest, so values within a block are distinct. Column 31 of each device holds z frequency -1. `colxy`: the columns are the 32 * 64 lattice columns nearest the z axis in the half plane (x frequency negative, or zero with y frequency zero or positive), ties in any order, dealt to the indices of ga; all values are distinct.
All inputs are finite; a program needn't handle non-finite values.
Results may differ from the reference program's by a relative error of at most 0.0025.
The reference program's roundings to bfloat16 on the way (of `updated` and `inverse`) count: a program that leaves them out, or rounds other values in their place, can miss the bound.
Values may be sent and summed in bfloat16 or wider, within the bound.
No kernel may reach another device: no remote copies, remote signals or barrier semaphores. Data moves between devices by JAX's collectives and lax.ppermute only.
A program may use at most 256 MiB of HBM per device.

```python
import jax
import jax.numpy as jnp
from jax import lax

NB = 1024
GDEV = 1408
NGRID = 128
COLS = 32
FB = 4
BAND_DEV = 256
NG = 90112
N_BAND = 4


def stick_layout(key):
    groups = NG // GDEV
    total_cols = COLS * groups
    plane = NGRID * NGRID
    cells = jnp.arange(plane, dtype=jnp.int32)
    xcell = cells // NGRID
    ycell = cells % NGRID
    xsign = jnp.where(xcell < NGRID // 2, xcell, xcell - NGRID)
    ysign = jnp.where(ycell < NGRID // 2, ycell, ycell - NGRID)
    radius_sq = xsign * xsign + ysign * ysign
    allowed = (xsign < 0) | (xsign == 0) & (ysign >= 0)
    tiebreak = jax.random.permutation(jax.random.fold_in(key, 101), plane).astype(jnp.int32)
    score = jnp.where(allowed, radius_sq * plane + tiebreak, jnp.int32(2 ** 30) + tiebreak)
    negated, picked = lax.top_k(-score, total_cols)
    picked = picked.astype(jnp.int32)
    stick_sq = radius_sq[picked]
    reach_sq = jnp.max(stick_sq)
    levels = jnp.arange(1, NGRID // 2, dtype=jnp.int32)
    height = jnp.sum(levels[None, :] * levels[None, :] + stick_sq[:, None] <= reach_sq, axis=1).astype(jnp.int32)
    base = 2 * height + 1
    order = jax.random.permutation(jax.random.fold_in(key, 103), groups).astype(jnp.int32)
    rank = jnp.arange(total_cols, dtype=jnp.int32)
    rounds = rank // groups
    within = rank % groups
    snake = jnp.where(rounds % 2 == 0, within, groups - 1 - within)
    owner = order[snake]
    column = COLS - 1 - rounds
    slot = owner * COLS + column
    colxy = jnp.zeros((total_cols,), jnp.int32).at[slot].set(picked)
    base_grid = jnp.zeros((total_cols,), jnp.int32).at[slot].set(base).reshape(groups, COLS)
    sums = jnp.sum(base_grid, axis=1, keepdims=True)
    spare = GDEV - COLS
    lengths = 1 + (base_grid - 1) * spare // jnp.maximum(sums - COLS, 1)
    left = GDEV - jnp.sum(lengths, axis=1, keepdims=True)
    col_ids = jnp.arange(COLS, dtype=jnp.int32)
    lengths = lengths + (col_ids[None, :] >= COLS - left).astype(jnp.int32)
    ends = jnp.cumsum(lengths, axis=1)
    starts = ends - lengths
    entries = jnp.arange(GDEV, dtype=jnp.int32)
    col_of = jnp.sum((entries[None, :, None] >= ends[:, None, :]).astype(jnp.int32), axis=2)
    start_of = jnp.take_along_axis(starts, col_of, axis=1)
    length_of = jnp.take_along_axis(lengths, col_of, axis=1)
    below = (length_of - 1) // 2
    zslot = (entries[None, :] - start_of - below) % NGRID
    gmap = (col_of * NGRID + zslot).reshape(NG).astype(jnp.int32)
    return (gmap, colxy)


def draw_gmap(key, part):
    layout = stick_layout(key)
    return layout[0]


def draw_colxy(key, part):
    layout = stick_layout(key)
    return layout[1]


def draw_psi(key, part):
    key = jax.random.fold_in(key, 5)
    noise_key, common_key, weight_key, scale_key = jax.random.split(key, 4)
    noise = jnp.clip(jax.random.normal(noise_key, (NB, 2, NG), jnp.float32), -6.0, 6.0)
    shared = 0.1
    scales = jnp.exp(jax.random.uniform(scale_key, (NB,), jnp.float32, jnp.log(0.4), jnp.log(4.0)))
    common = jnp.clip(jax.random.normal(common_key, (8, 2, NG), jnp.float32), -4.0, 4.0)
    weights = shared * jnp.clip(jax.random.normal(weight_key, (NB, 8), jnp.float32), -4.0, 4.0)
    total = noise
    for shared_index in range(8):
        total = total + weights[:, shared_index, None, None] * common[shared_index][None]
    total = jnp.clip(total, -8.0, 8.0)
    return (total * scales[:, None, None]).astype(jnp.bfloat16)


def block_scale(key, extent, cuts, smallest, high):
    def one(dim, parts):
        draws = jax.random.uniform(jax.random.fold_in(jax.random.fold_in(key, 6), dim), (parts,), jnp.float32, smallest / len(cuts), high / len(cuts))
        return jnp.repeat(jnp.exp(draws), extent[dim] // parts).reshape((-1,) + (1,) * (len(extent) - dim - 1))

    loudness = one(*cuts[0])
    for cut in cuts[1:]:
        loudness = loudness * one(*cut)
    return loudness


def setup_inputs(seed: int = 0) -> dict:
    key_list = jax.random.split(jax.random.key(seed), 5)
    return {
        "psi": draw_psi(jax.random.fold_in(key_list[4], 71), 0),
        "potential": jnp.clip(jax.random.uniform(key_list[1], (NGRID, NGRID, NGRID), jnp.float32, -5.0, 5.0) * block_scale(key_list[1], (NGRID, NGRID, NGRID), ((0, 64),), -0.4, 0.0), -5.0, 5.0),
        "gmap": draw_gmap(jax.random.fold_in(key_list[4], 71), 0),
        "colxy": draw_colxy(jax.random.fold_in(key_list[4], 71), 0),
    }


def signed_freq(values):
    as_float = values.astype(jnp.float32)
    return jnp.where(values < NGRID // 2, as_float, as_float - NGRID)

def reference(psi, potential, gmap, colxy):
    points = NGRID
    index = jnp.arange(NG, dtype=jnp.int32)
    column = index // GDEV * COLS + gmap // points
    zpos = gmap % points
    place = colxy[column]
    xpos = place // points
    ypos = place % points
    sx = signed_freq(xpos)
    sy = signed_freq(ypos)
    sz = signed_freq(zpos)
    kinetic = (sx * sx + sy * sy + sz * sz) * (32.0 / (points * points))
    blocks = psi.reshape(N_BAND, BAND_DEV, 2, NG)
    block = blocks[:, :FB].reshape(N_BAND * FB, 2, NG).astype(jnp.float32)
    volume = float(points) ** 3

    def apply_one(coeff):
        real_grid = jnp.zeros((points, points, points), jnp.float32).at[zpos, xpos, ypos].set(coeff[0])
        imag_grid = jnp.zeros((points, points, points), jnp.float32).at[zpos, xpos, ypos].set(coeff[1])
        field = 2.0 * jnp.real(jnp.fft.ifftn(lax.complex(real_grid, imag_grid))) * volume
        spectrum = jnp.fft.fftn(potential * field) / volume
        picked = spectrum[zpos, xpos, ypos]
        return jnp.stack([jnp.real(picked), jnp.imag(picked)])
    applied = lax.map(apply_one, block)
    hpsi = kinetic[None, None, :] * block + applied
    moved = (block - 0.25 * hpsi).astype(jnp.bfloat16)
    updated = blocks.at[:, :FB].set(moved.reshape(N_BAND, FB, 2, NG)).reshape(NB, 2 * NG)
    gram = jnp.dot(updated.astype(jnp.float32), updated.T.astype(jnp.float32), preferred_element_type=jnp.float32) * (2.0 / NG)
    lower = jnp.linalg.cholesky(gram)
    inverse = jax.scipy.linalg.solve_triangular(lower, jnp.eye(NB, dtype=jnp.float32), lower=True)
    inverse = inverse.astype(jnp.bfloat16)
    new_psi = jnp.dot(inverse.astype(jnp.float32), updated.astype(jnp.float32), preferred_element_type=jnp.float32).astype(jnp.bfloat16)
    return new_psi.reshape(NB, 2, NG)
```

```python
import functools
import math

import jax
import jax.numpy as jnp
from jax import lax
from jax.experimental import pallas as pl
from jax.experimental.pallas import tpu as pltpu
from jax.sharding import PartitionSpec as P


COLS = 32
FB = 4
HALF = 40
NT = (((1,), (1,)), ((), ()))
TN = (((0,), (0,)), ((), ()))
f32 = jnp.float32
bf16 = jnp.bfloat16


def tables(points):
    indices = jnp.arange(points, dtype=jnp.int32)
    phase = indices[:, None] * indices[None, :] % points
    angle = phase.astype(f32) * (2.0 * math.pi / points)
    return jnp.concatenate([jnp.cos(angle), jnp.sin(angle)], 0)


def split(x):
    high = x.astype(bf16)
    return high, (x - high.astype(f32)).astype(bf16)


def dot3(a, b, dims=(((1,), (0,)), ((), ()))):
    return lax.dot_general(a, b, dims, precision=lax.Precision.HIGH, preferred_element_type=f32)


def spread_kernel(psi_ref, gmap_ref, cs_ref, out_ref):
    gdev = psi_ref.shape[1]
    gmap = gmap_ref[...]
    col = gmap // 128
    zpos = gmap % 128
    colmask = lax.broadcasted_iota(jnp.int32, (COLS, gdev), 0) == col
    onez = (lax.broadcasted_iota(jnp.int32, (128, gdev), 0) == zpos).astype(f32).astype(bf16)
    psi = psi_ref[...].astype(f32)
    rows = [jnp.where(colmask, psi[2 * b + ri:2 * b + ri + 1, :], 0.0) for ri in range(2) for b in range(FB)]
    buf = lax.dot_general(jnp.concatenate(rows, 0).astype(bf16), onez, NT, preferred_element_type=f32)
    p = dot3(cs_ref[...], buf, NT)
    re = p[:128, :128] - p[128:, 128:]
    im = p[128:, :128] + p[:128, 128:]
    out_ref[...] = jnp.concatenate([re, im], 1).astype(bf16)


def plane_kernel(val_ref, colxy_ref, pot_ref, cs_ref, out_ref, g_ref, v_ref, wide):
    wide[...] = val_ref[...].astype(f32)
    ncols = val_ref.shape[1]
    place = colxy_ref[...]
    xneg = (128 - place // 128) % 128
    ypos = place % 128
    xmask = lax.broadcasted_iota(jnp.int32, (HALF, ncols), 0) == xneg
    oney = (lax.broadcasted_iota(jnp.int32, (128, ncols), 0) == ypos).astype(f32).astype(bf16)
    items = val_ref.shape[0]
    for j in range(items):
        a = jnp.where(xmask, wide[j:j + 1, :], 0.0).astype(bf16)
        g_ref[j * HALF:(j + 1) * HALF, :] = lax.dot_general(a, oney, NT, preferred_element_type=f32)
    cs = cs_ref[...]
    p = dot3(g_ref[...], cs, NT)
    xcs = jnp.concatenate([cs[:128, :HALF], cs[128:, :HALF]], 1)
    for zz in range(2):
        for b in range(FB):
            r0 = ((zz * 2) * FB + b) * HALF
            i0 = ((zz * 2 + 1) * FB + b) * HALF
            yr = p[r0:r0 + HALF, :128] - p[i0:i0 + HALF, 128:]
            yi = p[r0:r0 + HALF, 128:] + p[i0:i0 + HALF, :128]
            field = 2.0 * dot3(xcs, jnp.concatenate([yr, yi], 0))
            w = pot_ref[zz] * field
            v = dot3(xcs, w, TN)
            v_ref[r0:r0 + HALF, :] = v[:HALF]
            v_ref[i0:i0 + HALF, :] = v[HALF:]
    q = dot3(v_ref[...], cs, NT)
    for zz in range(2):
        for b in range(FB):
            r0 = ((zz * 2) * FB + b) * HALF
            i0 = ((zz * 2 + 1) * FB + b) * HALF
            re = q[r0:r0 + HALF, :128] + q[i0:i0 + HALF, 128:]
            im = q[i0:i0 + HALF, :128] - q[r0:r0 + HALF, 128:]
            for at, part in ((zz * 2 * FB + b, re), ((zz * 2 + 1) * FB + b, im)):
                t = jnp.dot((part * (2.0 ** -21)).astype(bf16), oney, preferred_element_type=f32)
                wide[at:at + 1, :] = jnp.sum(jnp.where(xmask, t, 0.0), 0, keepdims=True)
    out_ref[...] = wide[...].astype(bf16)


def collect_kernel(back_ref, psi_ref, gmap_ref, colt_ref, cs_ref, out_ref, wide):
    psi = psi_ref[...].astype(f32)
    gdev = psi_ref.shape[1]
    gmap = gmap_ref[...]
    col = gmap // 128
    zpos = gmap % 128
    colmask = lax.broadcasted_iota(jnp.int32, (COLS, gdev), 0) == col
    onez = (lax.broadcasted_iota(jnp.int32, (128, gdev), 0) == zpos).astype(f32).astype(bf16)

    def signed(v):
        return jnp.where(v < 64, v, v - 128).astype(f32)
    place = colt_ref[...]
    sx = signed(place // 128)
    sy = signed(place % 128)
    sz = signed(zpos)
    flat = jnp.sum(jnp.where(colmask, sx * sx + sy * sy, 0.0), 0, keepdims=True)
    kinetic = (flat + sz * sz) * (32.0 / (128 * 128))
    p = dot3(cs_ref[...], back_ref[...].astype(f32))
    re = p[:128, :128] + p[128:, 128:]
    im = p[:128, 128:] - p[128:, :128]
    for ri, spec in ((0, re), (1, im)):
        high, low = split(spec.T)
        t = jnp.dot(high, onez, preferred_element_type=f32) + jnp.dot(low, onez, preferred_element_type=f32)
        for b in range(FB):
            applied = jnp.sum(jnp.where(colmask, t[b * COLS:(b + 1) * COLS, :], 0.0), 0, keepdims=True)
            own = psi[2 * b + ri:2 * b + ri + 1, :]
            hpsi = kinetic * own + applied
            wide[2 * b + ri:2 * b + ri + 1, :] = own - 0.25 * hpsi
    out_ref[...] = wide[...].astype(bf16)


def vmem(n):
    return [pl.BlockSpec(memory_space=pltpu.VMEM)] * n


def call(kernel, shape, n, scratch=()):
    return pl.pallas_call(kernel, out_shape=jax.ShapeDtypeStruct(shape, bf16), in_specs=vmem(n), out_specs=vmem(1)[0],
                          scratch_shapes=list(scratch),
                          compiler_params=pltpu.CompilerParams(vmem_limit_bytes=48 << 20))


def spread(psi8, gmap, cs):
    return call(spread_kernel, (128, 256), 3)(psi8, gmap[None], cs)


def planes(val, colxy, potential, cs):
    rows = val.shape[0] * HALF
    return call(plane_kernel, val.shape, 4, [pltpu.VMEM((rows, 128), f32)] * 2 + [pltpu.VMEM(val.shape, f32)])(val, colxy[None], potential, cs)


def collect(back, psi8, gmap, place, cs):
    return call(collect_kernel, psi8.shape, 5, [pltpu.VMEM(psi8.shape, f32)])(back, psi8, gmap[None], place[:, None], cs)
HI = lax.Precision.HIGHEST
NN = (((1,), (0,)), ((), ()))


def mm(a, b, dims=NN):
    return lax.dot_general(a, b, dims, precision=HI, preferred_element_type=f32)


def factor_tile(tile):
    lane = lax.broadcasted_iota(jnp.int32, (8, 128), 1)
    sub = lax.broadcasted_iota(jnp.int32, (8, 128), 0)
    for p in range(16):
        r0 = 8 * p
        panel = tile[r0:r0 + 8, :]
        inside = (lane >= r0) & (lane < r0 + 8)
        cols = [jnp.broadcast_to(panel[:, r0 + k:r0 + k + 1], (8, 128)) for k in range(8)]
        a = {(i, k): jnp.broadcast_to(cols[k][i:i + 1, :], (8, 128)) for k in range(8) for i in range(k, 8)}
        l = {}
        r = []
        for k in range(8):
            rk = lax.rsqrt(a[k, k])
            r.append(rk)
            for i in range(k + 1, 8):
                l[i, k] = a[i, k] * rk
            for j in range(k + 1, 8):
                for i in range(j, 8):
                    a[i, j] = a[i, j] - l[i, k] * l[j, k]
        eye = jnp.where(lane - r0 == sub, 1.0, 0.0)
        start = jnp.where(inside, eye, panel)
        w = []
        out = jnp.zeros((8, 128), f32)
        for k in range(8):
            x = jnp.broadcast_to(start[k:k + 1, :], (8, 128))
            for m in range(k):
                x = x - l[k, m] * w[m]
            x = x * r[k]
            w.append(x)
            out = jnp.where(sub == k, x, out)
        tile[r0:r0 + 8, :] = out
        if p + 2 < 16:
            flip = out.T
        for i in range(p + 1, 16):
            row = tile[8 * i:8 * i + 8, :]
            rest = jnp.where(inside, 0.0, row)
            u = []
            for k in range(8):
                if i > p + DIRECT:
                    u.append(jnp.broadcast_to(flip[8 * i:8 * i + 8, k:k + 1], (8, 128)))
                    continue
                x = jnp.broadcast_to(row[:, r0 + k:r0 + k + 1], (8, 128))
                for m in range(k):
                    x = x - l[k, m] * u[m]
                u.append(x * r[k])
            for k in range(8):
                rest = rest - u[k] * w[k]
            tile[8 * i:8 * i + 8, :] = rest


DIRECT = 1


def factor(d, tile, tile2):
    lower = lax.broadcasted_iota(jnp.int32, (128, 128), 1) <= lax.broadcasted_iota(jnp.int32, (128, 128), 0)
    tile[...] = d[:128, :128]
    factor_tile(tile)
    first = jnp.where(lower, tile[...], 0.0)
    up = mm(first, d[:128, 128:])
    tile2[...] = d[128:, 128:] - mm(up, up, TN)
    cross = mm(up, first, TN)
    factor_tile(tile2)
    second = jnp.where(lower, tile2[...], 0.0)
    low = -mm(second, cross)
    return jnp.concatenate([jnp.concatenate([first, jnp.zeros((128, 128), f32)], 1), jnp.concatenate([low, second], 1)], 0)


def stage_kernel(stages, scale, meta_ref, *refs):
    b, c = meta_ref[0], meta_ref[1]
    refs = list(refs)
    halves = [refs.pop(0), refs.pop(0)]
    lead = {r: refs.pop(0) for r in range(stages[0])}
    last = stages[-1] == 3
    for r in stages:
        if not (last and r == stages[-1]):
            lead[r] = refs.pop(0)
    own = refs.pop(0) if last else None
    a_s, tile, tile2 = refs
    off = 0
    for r in stages:
        width = 256 * (r + 1)
        for h in range(2):
            for kb in range(4):
                at = 64 * ((b + kb) % 4) + 32 * (c if h == 0 else 1 - c)
                a_s[pl.ds(pl.multiple_of(at, 32), 32), 0:width] = halves[h][kb, :, off:off + width] * scale
        off += width
        d = a_s[:, 256 * r:width]
        w = []
        for j in range(r):
            w.append(mm(a_s[:, :256 * (j + 1)], lead[j][...], NT))
            d = d - mm(w[j], w[j], NT)
        v = [sum(mm(w[j], lead[j][:, 256 * i:256 * (i + 1)]) for j in range(i, r)) for i in range(r)]
        corner = factor(d, tile, tile2)
        row = jnp.concatenate([-mm(corner, v[i]) for i in range(r)] + [corner], 1) if r else corner
        if last and r == stages[-1]:
            for s in range(4):
                @pl.when(b == s)
                def _():
                    if s == r:
                        own[...] = row.astype(bf16)
                    else:
                        own[:, :256 * (s + 1)] = lead[s][...].astype(bf16)
                        own[:, 256 * (s + 1):] = jnp.zeros((256, 1024 - 256 * (s + 1)), bf16)
        else:
            lead[r][...] = row


def stage(stages, scale, meta, halves, lead):
    last = stages[-1] == 3
    shapes = [jax.ShapeDtypeStruct((256, 256 * (r + 1)), f32) for r in stages[:len(stages) - last]]
    if last:
        shapes.append(jax.ShapeDtypeStruct((256, 1024), bf16))
    return pl.pallas_call(
        functools.partial(stage_kernel, stages, scale),
        out_shape=shapes,
        in_specs=[pl.BlockSpec(memory_space=pltpu.SMEM)] + vmem(2 + len(lead)),
        out_specs=vmem(len(shapes)),
        scratch_shapes=[pltpu.VMEM((256, 1024), f32), pltpu.VMEM((128, 128), f32), pltpu.VMEM((128, 128), f32)],
        compiler_params=pltpu.CompilerParams(vmem_limit_bytes=32 << 20),
        cost_estimate=pl.CostEstimate(flops=10 ** 10 * len(stages), bytes_accessed=10 ** 7, transcendentals=0),
    )(meta, *halves, *lead)


def mates(n):
    return [[2 * a + c for a in range(n // 2)] for c in range(2)]


def from_core(v):
    n = lax.axis_size("ga")
    return lax.ppermute(v, "ga", [(g, g ^ 1) for g in range(n)])


def from_band(v, k):
    n = lax.axis_size("band")
    return lax.ppermute(v, "band", [(a, (a - k) % n) for a in range(n)])


def swap_mates(v):
    return lax.all_to_all(v, "ga", split_axis=0, concat_axis=0, tiled=True, axis_index_groups=mates(lax.axis_size("ga")))


def reduce_units(units, c):
    half = units.shape[0] // 2
    keep = lax.dynamic_slice_in_dim(units, c * half, half)
    give = lax.dynamic_slice_in_dim(units, (1 - c) * half, half)
    return jnp.sum(swap_mates(keep + from_core(give)), 0)


def spread_units(unit, half):
    return swap_mates(jnp.broadcast_to(unit[None], (half,) + unit.shape))


def spread_bands(rows):
    return jnp.stack([rows] + [from_band(rows, k) for k in range(1, 4)])


def shards(psi, potential, gmap, colxy):
    band_dev, _, gdev = psi.shape
    n_ga = lax.axis_size("ga")
    n_band = lax.axis_size("band")
    points = potential.shape[1]
    total_coeffs = gdev * n_ga
    scale = 2.0 / total_coeffs
    cs = tables(points)
    ga_index = lax.axis_index("ga")
    flat = psi.reshape(band_dev, 2 * gdev)
    band = lax.axis_index("band")
    c = ga_index % 2
    after, before = from_band(flat, 1), from_band(flat, -1)
    psi8 = psi[:FB].reshape(2 * FB, gdev)
    sent = spread(psi8, gmap, cs)
    received = lax.all_to_all(sent.reshape(n_ga, 2, 256), "ga", split_axis=0, concat_axis=0, tiled=True)
    val = received.reshape(n_ga, 16, COLS).transpose(1, 0, 2).reshape(16, n_ga * COLS)
    picked = planes(val, colxy, potential, cs)
    picked = picked.reshape(16, n_ga, COLS).transpose(1, 0, 2).reshape(n_ga, 2, 256)
    picked, after, before = lax.optimization_barrier((picked, after, before))
    cross = band_dev // 2
    across = from_band(after[:cross], 1), from_band(before[cross:], -1)
    back = lax.all_to_all(picked, "ga", split_axis=0, concat_axis=0, tiled=True)
    own_columns = lax.dynamic_slice_in_dim(colxy, ga_index * COLS, COLS)
    moved = collect(back.reshape(2 * n_ga, 256), psi8, gmap, own_columns, cs).reshape(FB, 2 * gdev)

    every = jnp.zeros((n_band, band_dev, 2 * gdev), bf16)
    for part, k, at in ((flat, 0, 0), (after, 1, 0), (before, 3, 0), (across[0], 2, 0), (across[1], 2, cross)):
        every = lax.dynamic_update_slice(every, part[None], ((band + k) % n_band, at, 0))
    for k in range(n_band):
        rows = from_band(moved, k) if k else moved
        every = lax.dynamic_update_slice(every, rows[None], ((band + k) % n_band, 0, 0))
    strip = band_dev // n_band
    own = lax.dynamic_slice(every, (0, band * strip, 0), (n_band, strip, 2 * gdev)).reshape(band_dev, 2 * gdev)
    every = every.reshape(n_band * band_dev, 2 * gdev)
    part = lax.dot_general(own, every, NT, preferred_element_type=f32).reshape(n_band, strip, n_band * band_dev)
    units = jnp.concatenate([part[r, :, :band_dev * (r + 1)] for r in range(n_band)], 1).reshape(strip, -1, 128)
    rows = spread_units(reduce_units(units, c), strip // 2)
    cut = 3 * band_dev // 128
    meta = jnp.stack([band, c]).astype(jnp.int32)
    first = spread_bands(rows[:, :cut].reshape(strip // 2, -1))
    first, rest = lax.optimization_barrier((first, rows[:, cut:].reshape(strip // 2, -1)))
    parts = [from_band(rest, k) for k in range(1, n_band)]
    lead = stage((0, 1), scale, meta, (first, from_core(first)), [])
    parts, lead = lax.optimization_barrier((parts, lead))
    second = jnp.stack([rest, *parts])
    own_rows = stage((2, 3), scale, meta, (second, from_core(second)), lead)[-1]
    rotated = jnp.dot(own_rows, every, preferred_element_type=f32)
    return rotated.astype(bf16).reshape(band_dev, 2, gdev)


def solution(mesh):
    in_specs = (P("band", None, "ga"), P("ga", None, None), P("ga"), P())
    out_specs = P("band", None, "ga")
    return jax.shard_map(shards, mesh=mesh, in_specs=in_specs, out_specs=out_specs, check_vma=False)
```

```python
import functools
import math

import jax
import jax.numpy as jnp
from jax import lax
from jax.experimental import pallas as pl
from jax.experimental.pallas import tpu as pltpu
from jax.sharding import PartitionSpec as P


COLS = 32
FB = 4
HALF = 40
NT = (((1,), (1,)), ((), ()))
TN = (((0,), (0,)), ((), ()))
f32 = jnp.float32
bf16 = jnp.bfloat16


def tables(points):
    indices = jnp.arange(points, dtype=jnp.int32)
    phase = indices[:, None] * indices[None, :] % points
    angle = phase.astype(f32) * (2.0 * math.pi / points)
    return jnp.concatenate([jnp.cos(angle), jnp.sin(angle)], 0)


def split(x):
    high = x.astype(bf16)
    return high, (x - high.astype(f32)).astype(bf16)


def dot3(a, b, dims=(((1,), (0,)), ((), ()))):
    return lax.dot_general(a, b, dims, precision=lax.Precision.HIGH, preferred_element_type=f32)


def dot1(a, b, dims=(((1,), (0,)), ((), ()))):
    return lax.dot_general(a.astype(bf16), b.astype(bf16), dims, preferred_element_type=f32)


def spread_kernel(psi_ref, gmap_ref, cs_ref, out_ref):
    gdev = psi_ref.shape[1]
    gmap = gmap_ref[...]
    col = gmap // 128
    zpos = gmap % 128
    colmask = lax.broadcasted_iota(jnp.int32, (COLS, gdev), 0) == col
    onez = (lax.broadcasted_iota(jnp.int32, (128, gdev), 0) == zpos).astype(f32).astype(bf16)
    psi = psi_ref[...].astype(f32)
    rows = [jnp.where(colmask, psi[2 * b + ri:2 * b + ri + 1, :], 0.0) for ri in range(2) for b in range(FB)]
    buf = lax.dot_general(jnp.concatenate(rows, 0).astype(bf16), onez, NT, preferred_element_type=f32)
    p = dot3(cs_ref[...], buf, NT)
    re = p[:128, :128] - p[128:, 128:]
    im = p[128:, :128] + p[:128, 128:]
    out_ref[...] = jnp.concatenate([re, im], 1).astype(bf16)


def plane_kernel(val_ref, colxy_ref, pot_ref, cs_ref, out_ref, g_ref, v_ref, wide):
    wide[...] = val_ref[...].astype(f32)
    ncols = val_ref.shape[1]
    place = colxy_ref[...]
    xneg = (128 - place // 128) % 128
    ypos = place % 128
    xmask = lax.broadcasted_iota(jnp.int32, (HALF, ncols), 0) == xneg
    oney = (lax.broadcasted_iota(jnp.int32, (128, ncols), 0) == ypos).astype(f32).astype(bf16)
    items = val_ref.shape[0]
    for j in range(items):
        a = jnp.where(xmask, wide[j:j + 1, :], 0.0).astype(bf16)
        g_ref[j * HALF:(j + 1) * HALF, :] = lax.dot_general(a, oney, NT, preferred_element_type=f32)
    cs = cs_ref[...]
    p = dot1(g_ref[...], cs, NT)
    xcs = jnp.concatenate([cs[:128, :HALF], cs[128:, :HALF]], 1)
    for zz in range(2):
        for b in range(FB):
            r0 = ((zz * 2) * FB + b) * HALF
            i0 = ((zz * 2 + 1) * FB + b) * HALF
            yr = p[r0:r0 + HALF, :128] - p[i0:i0 + HALF, 128:]
            yi = p[r0:r0 + HALF, 128:] + p[i0:i0 + HALF, :128]
            field = 2.0 * dot1(xcs, jnp.concatenate([yr, yi], 0))
            w = pot_ref[zz] * field
            v = dot1(xcs, w, TN)
            v_ref[r0:r0 + HALF, :] = v[:HALF]
            v_ref[i0:i0 + HALF, :] = v[HALF:]
    q = dot1(v_ref[...], cs, NT)
    for zz in range(2):
        for b in range(FB):
            r0 = ((zz * 2) * FB + b) * HALF
            i0 = ((zz * 2 + 1) * FB + b) * HALF
            re = q[r0:r0 + HALF, :128] + q[i0:i0 + HALF, 128:]
            im = q[i0:i0 + HALF, :128] - q[r0:r0 + HALF, 128:]
            for at, part in ((zz * 2 * FB + b, re), ((zz * 2 + 1) * FB + b, im)):
                t = jnp.dot((part * (2.0 ** -21)).astype(bf16), oney, preferred_element_type=f32)
                wide[at:at + 1, :] = jnp.sum(jnp.where(xmask, t, 0.0), 0, keepdims=True)
    out_ref[...] = wide[...].astype(bf16)


def collect_kernel(back_ref, psi_ref, gmap_ref, colt_ref, cs_ref, out_ref, wide):
    psi = psi_ref[...].astype(f32)
    gdev = psi_ref.shape[1]
    gmap = gmap_ref[...]
    col = gmap // 128
    zpos = gmap % 128
    colmask = lax.broadcasted_iota(jnp.int32, (COLS, gdev), 0) == col
    onez = (lax.broadcasted_iota(jnp.int32, (128, gdev), 0) == zpos).astype(f32).astype(bf16)

    def signed(v):
        return jnp.where(v < 64, v, v - 128).astype(f32)
    place = colt_ref[...]
    sx = signed(place // 128)
    sy = signed(place % 128)
    sz = signed(zpos)
    flat = jnp.sum(jnp.where(colmask, sx * sx + sy * sy, 0.0), 0, keepdims=True)
    kinetic = (flat + sz * sz) * (32.0 / (128 * 128))
    p = dot3(cs_ref[...], back_ref[...].astype(f32))
    re = p[:128, :128] + p[128:, 128:]
    im = p[:128, 128:] - p[128:, :128]
    for ri, spec in ((0, re), (1, im)):
        high, low = split(spec.T)
        t = jnp.dot(high, onez, preferred_element_type=f32) + jnp.dot(low, onez, preferred_element_type=f32)
        for b in range(FB):
            applied = jnp.sum(jnp.where(colmask, t[b * COLS:(b + 1) * COLS, :], 0.0), 0, keepdims=True)
            own = psi[2 * b + ri:2 * b + ri + 1, :]
            hpsi = kinetic * own + applied
            wide[2 * b + ri:2 * b + ri + 1, :] = own - 0.25 * hpsi
    out_ref[...] = wide[...].astype(bf16)


def vmem(n):
    return [pl.BlockSpec(memory_space=pltpu.VMEM)] * n


def call(kernel, shape, n, scratch=()):
    return pl.pallas_call(kernel, out_shape=jax.ShapeDtypeStruct(shape, bf16), in_specs=vmem(n), out_specs=vmem(1)[0],
                          scratch_shapes=list(scratch),
                          compiler_params=pltpu.CompilerParams(vmem_limit_bytes=48 << 20))


def spread(psi8, gmap, cs):
    return call(spread_kernel, (128, 256), 3)(psi8, gmap[None], cs)


def planes(val, colxy, potential, cs):
    rows = val.shape[0] * HALF
    return call(plane_kernel, val.shape, 4, [pltpu.VMEM((rows, 128), f32)] * 2 + [pltpu.VMEM(val.shape, f32)])(val, colxy[None], potential, cs)


def collect(back, psi8, gmap, place, cs):
    return call(collect_kernel, psi8.shape, 5, [pltpu.VMEM(psi8.shape, f32)])(back, psi8, gmap[None], place[:, None], cs)


PIECES = ((0, 0, 2), (1, 0, 1), (1, 1, 1), (3, 0, 1), (3, 1, 1), (2, 0, 1), (2, 1, 1))


def fetches(b, refs, held, sem, cut=slice(None), row=()):
    per = held.shape[0] // 4
    out = []
    for i, (ref, (k, low, n)) in enumerate(zip(refs, PIECES)):
        start = pl.multiple_of((b + k) % 4 * per + low * (per // 2), per // 2)
        out.append(pltpu.make_async_copy(ref.at[:, cut], held.at[pl.ds(start, n * per // 2), cut], sem.at[(*row, i)]))
    return out


def refresh(b, fresh, held, cut, width):
    per = held.shape[0] // 4
    new = lax.broadcasted_iota(jnp.int32, (16, width), 0) < FB
    for k in range(4):
        at = pl.ds(pl.multiple_of((b + k) % 4 * per, per), 16)
        held[at, cut] = jnp.where(new, fresh[16 * k:16 * k + 16, cut].astype(f32), held[at, cut].astype(f32)).astype(bf16)


def gram_kernel(band_ref, *refs):
    pieces = refs[:len(PIECES)]
    fresh, units_ref, held, sem = refs[len(PIECES):]
    b = band_ref[0]
    n, width = held.shape
    per = n // 4
    strip = per // 4
    first = width // 512 * 256
    cuts = ((0, first), (first, width - first))
    copies = [fetches(b, pieces, held, sem, pl.ds(*cut), (h,)) for h, cut in enumerate(cuts)]
    for copy in copies[0] + copies[1]:
        copy.start()
    total = None
    for h, (start, size) in enumerate(cuts):
        for copy in copies[h]:
            copy.wait()
        cut = pl.ds(start, size)
        refresh(b, fresh, held, cut, size)
        lhs = jnp.concatenate([held[pl.ds(pl.multiple_of(r * per + b * strip, strip), strip), cut] for r in range(4)], 0)
        part = lax.dot_general(lhs, held[:, cut], NT, preferred_element_type=f32)
        total = part if total is None else total + part
    off = 0
    for r in range(4):
        units_ref[:, off:off + per * (r + 1)] = total[strip * r:strip * (r + 1), :per * (r + 1)]
        off += per * (r + 1)


def gram(band, parts, moved):
    per, width = parts[0].shape
    n = 4 * per
    return pl.pallas_call(
        gram_kernel,
        out_shape=jax.ShapeDtypeStruct((per // 4, 10 * per), f32),
        in_specs=[pl.BlockSpec(memory_space=pltpu.SMEM)] + [pl.BlockSpec(memory_space=pl.ANY)] * len(parts) + vmem(1),
        out_specs=vmem(1)[0],
        scratch_shapes=[pltpu.VMEM((n, width), bf16), pltpu.SemaphoreType.DMA((2, len(parts)))],
        compiler_params=pltpu.CompilerParams(vmem_limit_bytes=24 << 20),
        cost_estimate=pl.CostEstimate(flops=2 * per * n * width, bytes_accessed=2 * n * width, transcendentals=0),
    )(band, *parts, moved)
HI = lax.Precision.HIGHEST
NN = (((1,), (0,)), ((), ()))


def mm(a, b, dims=NN):
    return lax.dot_general(a, b, dims, precision=HI, preferred_element_type=f32)


def factor_tile(tile):
    lane = lax.broadcasted_iota(jnp.int32, (8, 128), 1)
    sub = lax.broadcasted_iota(jnp.int32, (8, 128), 0)
    for p in range(16):
        r0 = 8 * p
        panel = tile[r0:r0 + 8, :]
        inside = (lane >= r0) & (lane < r0 + 8)
        cols = [jnp.broadcast_to(panel[:, r0 + k:r0 + k + 1], (8, 128)) for k in range(8)]
        a = {(i, k): jnp.broadcast_to(cols[k][i:i + 1, :], (8, 128)) for k in range(8) for i in range(k, 8)}
        l = {}
        r = []
        for k in range(8):
            rk = lax.rsqrt(a[k, k])
            r.append(rk)
            for i in range(k + 1, 8):
                l[i, k] = a[i, k] * rk
            for j in range(k + 1, 8):
                for i in range(j, 8):
                    a[i, j] = a[i, j] - l[i, k] * l[j, k]
        eye = jnp.where(lane - r0 == sub, 1.0, 0.0)
        start = jnp.where(inside, eye, panel)
        w = []
        out = jnp.zeros((8, 128), f32)
        for k in range(8):
            x = jnp.broadcast_to(start[k:k + 1, :], (8, 128))
            for m in range(k):
                x = x - l[k, m] * w[m]
            x = x * r[k]
            w.append(x)
            out = jnp.where(sub == k, x, out)
        tile[r0:r0 + 8, :] = out
        if p % 8 + 2 < 8:
            flip = out.T
        for i in range(p + 1, 8 if p < 8 else 16):
            row = tile[8 * i:8 * i + 8, :]
            rest = jnp.where(inside, 0.0, row)
            u = []
            for k in range(8):
                if i > p + DIRECT:
                    u.append(jnp.broadcast_to(flip[8 * i:8 * i + 8, k:k + 1], (8, 128)))
                    continue
                x = jnp.broadcast_to(row[:, r0 + k:r0 + k + 1], (8, 128))
                for m in range(k):
                    x = x - l[k, m] * u[m]
                u.append(x * r[k])
            for k in range(8):
                rest = rest - u[k] * w[k]
            tile[8 * i:8 * i + 8, :] = rest
        if p == 7:
            top = tile[:64, :]
            row = lax.broadcasted_iota(jnp.int32, (64, 128), 0)
            col = lax.broadcasted_iota(jnp.int32, (64, 128), 1)
            done = jnp.where((col <= row) | (col >= 64), top, 0.0)
            tile[64:, :] = jnp.where(col < 64, 0.0, tile[64:, :]) - mm(top[:, 64:], done, TN)


DIRECT = 1


def factor(d, tile, tile2):
    lower = lax.broadcasted_iota(jnp.int32, (128, 128), 1) <= lax.broadcasted_iota(jnp.int32, (128, 128), 0)
    tile[...] = d[:128, :128]
    factor_tile(tile)
    first = jnp.where(lower, tile[...], 0.0)
    up = mm(first, d[:128, 128:])
    tile2[...] = d[128:, 128:] - mm(up, up, TN)
    cross = mm(up, first, TN)
    factor_tile(tile2)
    second = jnp.where(lower, tile2[...], 0.0)
    low = -mm(second, cross)
    return jnp.concatenate([jnp.concatenate([first, jnp.zeros((128, 128), f32)], 1), jnp.concatenate([low, second], 1)], 0)


def stage_kernel(stages, scale, meta_ref, *refs):
    b, c = meta_ref[0], meta_ref[1]
    refs = list(refs)
    last = stages[-1] == 3
    if last:
        held, own, sem = refs.pop(), refs.pop(), refs.pop()
        pieces = [refs.pop(0) for _ in PIECES]
        fresh = refs.pop(0)
        copies = fetches(b, pieces, held, sem)
        for copy in copies:
            copy.start()
    halves = [refs.pop(0), refs.pop(0)]
    lead = {r: refs.pop(0) for r in range(stages[0])}
    for r in stages:
        if not (last and r == stages[-1]):
            lead[r] = refs.pop(0)
    out = refs.pop(0) if last else None
    a_s, tile, tile2 = refs
    off = 0
    for r in stages:
        width = 256 * (r + 1)
        for h in range(2):
            for kb in range(4):
                at = 64 * ((b + kb) % 4) + 32 * (c if h == 0 else 1 - c)
                a_s[pl.ds(pl.multiple_of(at, 32), 32), 0:width] = halves[h][kb, :, off:off + width] * scale
        off += width
        d = a_s[:, 256 * r:width]
        w = []
        for j in range(r):
            w.append(mm(a_s[:, :256 * (j + 1)], lead[j][...], NT))
            d = d - mm(w[j], w[j], NT)
        v = [sum(mm(w[j], lead[j][:, 256 * i:256 * (i + 1)]) for j in range(i, r)) for i in range(r)]
        corner = factor(d, tile, tile2)
        row = jnp.concatenate([-mm(corner, v[i]) for i in range(r)] + [corner], 1) if r else corner
        if last and r == stages[-1]:
            for s in range(4):
                @pl.when(b == s)
                def _():
                    if s == r:
                        own[...] = row.astype(bf16)
                    else:
                        own[:, :256 * (s + 1)] = lead[s][...].astype(bf16)
                        own[:, 256 * (s + 1):] = jnp.zeros((256, 1024 - 256 * (s + 1)), bf16)
        else:
            lead[r][...] = row
    if last:
        for copy in copies:
            copy.wait()
        refresh(b, fresh, held, slice(None), held.shape[1])
        for at in range(0, out.shape[1], 256):
            out[:, at:at + 256] = jnp.dot(own[...], held[:, at:at + 256], preferred_element_type=f32).astype(bf16)


def stage(stages, scale, meta, halves, lead, parts=(), fresh=None):
    last = stages[-1] == 3
    shapes = [jax.ShapeDtypeStruct((256, 256 * (r + 1)), f32) for r in stages[:len(stages) - last]]
    scratch = [pltpu.VMEM((256, 1024), f32), pltpu.VMEM((128, 128), f32), pltpu.VMEM((128, 128), f32)]
    if last:
        shapes.append(jax.ShapeDtypeStruct((256, fresh.shape[1]), bf16))
        scratch += [pltpu.SemaphoreType.DMA((len(parts),)), pltpu.VMEM((256, 1024), bf16), pltpu.VMEM((1024, fresh.shape[1]), bf16)]
    return pl.pallas_call(
        functools.partial(stage_kernel, stages, scale),
        out_shape=shapes,
        in_specs=[pl.BlockSpec(memory_space=pltpu.SMEM)] + [pl.BlockSpec(memory_space=pl.ANY)] * len(parts) + vmem(2 + len(lead) + last),
        out_specs=vmem(len(shapes)),
        scratch_shapes=scratch,
        compiler_params=pltpu.CompilerParams(vmem_limit_bytes=28 << 20),
        cost_estimate=pl.CostEstimate(flops=10 ** 10 * len(stages), bytes_accessed=10 ** 7, transcendentals=0),
    )(meta, *parts, *([fresh] if last else []), *halves, *lead)


def mates(n):
    return [[2 * a + c for a in range(n // 2)] for c in range(2)]


def from_core(v):
    n = lax.axis_size("ga")
    return lax.ppermute(v, "ga", [(g, g ^ 1) for g in range(n)])


def from_band(v, k):
    n = lax.axis_size("band")
    return lax.ppermute(v, "band", [(a, (a - k) % n) for a in range(n)])


def swap_mates(v):
    return lax.all_to_all(v, "ga", split_axis=0, concat_axis=0, tiled=True, axis_index_groups=mates(lax.axis_size("ga")))


def reduce_units(units, c):
    half = units.shape[0] // 2
    keep = lax.dynamic_slice_in_dim(units, c * half, half)
    give = lax.dynamic_slice_in_dim(units, (1 - c) * half, half)
    return jnp.sum(swap_mates(keep + from_core(give)), 0)


def spread_units(unit, half):
    return swap_mates(jnp.broadcast_to(unit[None], (half,) + unit.shape))


def spread_bands(rows):
    return jnp.stack([rows] + [from_band(rows, k) for k in range(1, 4)])


def shards(psi, potential, gmap, colxy):
    band_dev, _, gdev = psi.shape
    n_ga = lax.axis_size("ga")
    n_band = lax.axis_size("band")
    points = potential.shape[1]
    scale = 2.0 / (gdev * n_ga)
    cs = tables(points)
    ga_index = lax.axis_index("ga")
    band = lax.axis_index("band")
    c = ga_index % 2
    flat = lax.optimization_barrier(psi.reshape(band_dev, 2 * gdev))
    cross = band_dev // 2
    low, high = flat[:cross], flat[cross:]
    after_low, before_high = from_band(low, 1), from_band(high, -1)
    after_high, before_low = from_band(high, 1), from_band(low, -1)
    psi8 = psi[:FB].reshape(2 * FB, gdev)
    sent = spread(psi8, gmap, cs).reshape(n_ga, 2, 256)
    received = lax.all_to_all(sent, "ga", split_axis=0, concat_axis=0, tiled=True)
    received, after_low, before_high = lax.optimization_barrier((received, after_low, before_high))
    far_low, far_high = from_band(after_low, 1), from_band(before_high, -1)
    val = received.reshape(n_ga, 16, COLS).transpose(1, 0, 2).reshape(16, n_ga * COLS)
    picked = planes(val, colxy, potential, cs)
    picked = picked.reshape(16, n_ga, COLS).transpose(1, 0, 2).reshape(n_ga, 2, 256)
    back = lax.all_to_all(picked, "ga", split_axis=0, concat_axis=0, tiled=True)
    own_columns = lax.dynamic_slice_in_dim(colxy, ga_index * COLS, COLS)
    moved = collect(back.reshape(2 * n_ga, 256), psi8, gmap, own_columns, cs).reshape(FB, 2 * gdev)
    moved, after_high, before_low, far_low, far_high = lax.optimization_barrier((moved, after_high, before_low, far_low, far_high))
    fresh = jnp.stack([moved] + [from_band(moved, k) for k in range(1, n_band)])
    fresh = jnp.pad(fresh, ((0, 0), (0, 16 - FB), (0, 0))).reshape(n_band * 16, 2 * gdev)
    pieces = (flat, after_low, after_high, before_low, before_high, far_low, far_high)
    units = gram(band.astype(jnp.int32)[None], pieces, fresh)
    strip = band_dev // n_band
    rows = spread_units(reduce_units(units.reshape(strip, -1, 128), c), strip // 2)
    meta = jnp.stack([band, c]).astype(jnp.int32)
    cut = sum(range(1, SPLIT + 1)) * band_dev // 128
    first = spread_bands(rows[:, :cut].reshape(strip // 2, -1))
    first, rest = lax.optimization_barrier((first, rows[:, cut:].reshape(strip // 2, -1)))
    parts = [from_band(rest, k) for k in range(1, n_band)]
    lead = stage(tuple(range(SPLIT)), scale, meta, (first, from_core(first)), [])
    parts, lead = lax.optimization_barrier((parts, lead))
    second = jnp.stack([rest, *parts])
    rotated = stage(tuple(range(SPLIT, n_band)), scale, meta, (second, from_core(second)), lead, pieces, fresh)[-1]
    return rotated.reshape(band_dev, 2, gdev)


SPLIT = 2


def solution(mesh):
    in_specs = (P("band", None, "ga"), P("ga", None, None), P("ga"), P())
    out_specs = P("band", None, "ga")
    return jax.shard_map(shards, mesh=mesh, in_specs=in_specs, out_specs=out_specs, check_vma=False)
```

```python
import functools
import math

import jax
import jax.numpy as jnp
from jax import lax
from jax.experimental import pallas as pl
from jax.experimental.pallas import tpu as pltpu
from jax.sharding import PartitionSpec as P


COLS = 32
FB = 4
HALF = 40
NT = (((1,), (1,)), ((), ()))
TN = (((0,), (0,)), ((), ()))
f32 = jnp.float32
bf16 = jnp.bfloat16


def tables(points):
    indices = jnp.arange(points, dtype=jnp.int32)
    phase = indices[:, None] * indices[None, :] % points
    angle = phase.astype(f32) * (2.0 * math.pi / points)
    return jnp.concatenate([jnp.cos(angle), jnp.sin(angle)], 0)


def split(x):
    high = x.astype(bf16)
    return high, (x - high.astype(f32)).astype(bf16)


def dot3(a, b, dims=(((1,), (0,)), ((), ()))):
    return lax.dot_general(a, b, dims, precision=lax.Precision.HIGH, preferred_element_type=f32)


def dot1(a, b, dims=(((1,), (0,)), ((), ()))):
    return lax.dot_general(a.astype(bf16), b.astype(bf16), dims, preferred_element_type=f32)


def spread_kernel(psi_ref, gmap_ref, cs_ref, out_ref):
    gdev = psi_ref.shape[1]
    gmap = gmap_ref[...]
    col = gmap // 128
    zpos = gmap % 128
    colmask = lax.broadcasted_iota(jnp.int32, (COLS, gdev), 0) == col
    onez = (lax.broadcasted_iota(jnp.int32, (128, gdev), 0) == zpos).astype(f32).astype(bf16)
    psi = psi_ref[...].astype(f32)
    rows = [jnp.where(colmask, psi[2 * b + ri:2 * b + ri + 1, :], 0.0) for ri in range(2) for b in range(FB)]
    buf = lax.dot_general(jnp.concatenate(rows, 0).astype(bf16), onez, NT, preferred_element_type=f32)
    p = dot3(cs_ref[...], buf, NT)
    re = p[:128, :128] - p[128:, 128:]
    im = p[128:, :128] + p[:128, 128:]
    out_ref[...] = jnp.concatenate([re, im], 1).astype(bf16)


def plane_kernel(val_ref, colxy_ref, pot_ref, cs_ref, out_ref, g_ref, v_ref, wide):
    wide[...] = val_ref[...].astype(f32)
    ncols = val_ref.shape[1]
    place = colxy_ref[...]
    xneg = (128 - place // 128) % 128
    ypos = place % 128
    xmask = lax.broadcasted_iota(jnp.int32, (HALF, ncols), 0) == xneg
    oney = (lax.broadcasted_iota(jnp.int32, (128, ncols), 0) == ypos).astype(f32).astype(bf16)
    items = val_ref.shape[0]
    for j in range(items):
        a = jnp.where(xmask, wide[j:j + 1, :], 0.0).astype(bf16)
        g_ref[j * HALF:(j + 1) * HALF, :] = lax.dot_general(a, oney, NT, preferred_element_type=f32)
    cs = cs_ref[...]
    p = dot1(g_ref[...], cs, NT)
    xcs = jnp.concatenate([cs[:128, :HALF], cs[128:, :HALF]], 1)
    for zz in range(2):
        for b in range(FB):
            r0 = ((zz * 2) * FB + b) * HALF
            i0 = ((zz * 2 + 1) * FB + b) * HALF
            yr = p[r0:r0 + HALF, :128] - p[i0:i0 + HALF, 128:]
            yi = p[r0:r0 + HALF, 128:] + p[i0:i0 + HALF, :128]
            field = 2.0 * dot1(xcs, jnp.concatenate([yr, yi], 0))
            w = pot_ref[zz] * field
            v = dot1(xcs, w, TN)
            v_ref[r0:r0 + HALF, :] = v[:HALF]
            v_ref[i0:i0 + HALF, :] = v[HALF:]
    q = dot1(v_ref[...], cs, NT)
    for zz in range(2):
        for b in range(FB):
            r0 = ((zz * 2) * FB + b) * HALF
            i0 = ((zz * 2 + 1) * FB + b) * HALF
            re = q[r0:r0 + HALF, :128] + q[i0:i0 + HALF, 128:]
            im = q[i0:i0 + HALF, :128] - q[r0:r0 + HALF, 128:]
            for at, part in ((zz * 2 * FB + b, re), ((zz * 2 + 1) * FB + b, im)):
                t = jnp.dot((part * (2.0 ** -21)).astype(bf16), oney, preferred_element_type=f32)
                wide[at:at + 1, :] = jnp.sum(jnp.where(xmask, t, 0.0), 0, keepdims=True)
    out_ref[...] = wide[...].astype(bf16)


def collect_kernel(back_ref, psi_ref, gmap_ref, colt_ref, cs_ref, out_ref, wide):
    psi = psi_ref[...].astype(f32)
    gdev = psi_ref.shape[1]
    gmap = gmap_ref[...]
    col = gmap // 128
    zpos = gmap % 128
    colmask = lax.broadcasted_iota(jnp.int32, (COLS, gdev), 0) == col
    onez = (lax.broadcasted_iota(jnp.int32, (128, gdev), 0) == zpos).astype(f32).astype(bf16)

    def signed(v):
        return jnp.where(v < 64, v, v - 128).astype(f32)
    place = colt_ref[...]
    sx = signed(place // 128)
    sy = signed(place % 128)
    sz = signed(zpos)
    flat = jnp.sum(jnp.where(colmask, sx * sx + sy * sy, 0.0), 0, keepdims=True)
    kinetic = (flat + sz * sz) * (32.0 / (128 * 128))
    p = dot3(cs_ref[...], back_ref[...].astype(f32))
    re = p[:128, :128] + p[128:, 128:]
    im = p[:128, 128:] - p[128:, :128]
    for ri, spec in ((0, re), (1, im)):
        high, low = split(spec.T)
        t = jnp.dot(high, onez, preferred_element_type=f32) + jnp.dot(low, onez, preferred_element_type=f32)
        for b in range(FB):
            applied = jnp.sum(jnp.where(colmask, t[b * COLS:(b + 1) * COLS, :], 0.0), 0, keepdims=True)
            own = psi[2 * b + ri:2 * b + ri + 1, :]
            hpsi = kinetic * own + applied
            wide[2 * b + ri:2 * b + ri + 1, :] = own - 0.25 * hpsi
    out_ref[...] = wide[...].astype(bf16)


def vmem(n):
    return [pl.BlockSpec(memory_space=pltpu.VMEM)] * n


def call(kernel, shape, n, scratch=()):
    return pl.pallas_call(kernel, out_shape=jax.ShapeDtypeStruct(shape, bf16), in_specs=vmem(n), out_specs=vmem(1)[0],
                          scratch_shapes=list(scratch),
                          compiler_params=pltpu.CompilerParams(vmem_limit_bytes=48 << 20))


def spread(psi8, gmap, cs):
    return call(spread_kernel, (128, 256), 3)(psi8, gmap[None], cs)


def planes(val, colxy, potential, cs):
    rows = val.shape[0] * HALF
    return call(plane_kernel, val.shape, 4, [pltpu.VMEM((rows, 128), f32)] * 2 + [pltpu.VMEM(val.shape, f32)])(val, colxy[None], potential, cs)


def collect(back, psi8, gmap, place, cs):
    return call(collect_kernel, psi8.shape, 5, [pltpu.VMEM(psi8.shape, f32)])(back, psi8, gmap[None], place[:, None], cs)


PIECES = ((0, 0, 2), (1, 0, 1), (1, 1, 1), (3, 0, 1), (3, 1, 1), (2, 0, 1), (2, 1, 1))


def fetches(b, refs, held, sem, cut=slice(None), row=()):
    per = held.shape[0] // 4
    out = []
    for i, (ref, (k, low, n)) in enumerate(zip(refs, PIECES)):
        start = pl.multiple_of((b + k) % 4 * per + low * (per // 2), per // 2)
        out.append(pltpu.make_async_copy(ref.at[:, cut], held.at[pl.ds(start, n * per // 2), cut], sem.at[(*row, i)]))
    return out


def refresh(b, fresh, held, cut, width):
    per = held.shape[0] // 4
    new = lax.broadcasted_iota(jnp.int32, (16, width), 0) < FB
    for k in range(4):
        at = pl.ds(pl.multiple_of((b + k) % 4 * per, per), 16)
        held[at, cut] = jnp.where(new, fresh[16 * k:16 * k + 16, cut].astype(f32), held[at, cut].astype(f32)).astype(bf16)


def gram_kernel(band_ref, *refs):
    pieces = refs[:len(PIECES)]
    fresh, keep_ref, give_ref, held, sem = refs[len(PIECES):]
    b, c = band_ref[0], band_ref[1]
    n, width = held.shape
    per = n // 4
    strip = per // 4
    first = width // 512 * 256
    cuts = ((0, first), (first, width - first))
    copies = [fetches(b, pieces, held, sem, pl.ds(*cut), (h,)) for h, cut in enumerate(cuts)]
    for copy in copies[0] + copies[1]:
        copy.start()
    total = None
    for h, (start, size) in enumerate(cuts):
        for copy in copies[h]:
            copy.wait()
        cut = pl.ds(start, size)
        refresh(b, fresh, held, cut, size)
        starts = [r * per + b * strip + core * (strip // 2) for r in range(4) for core in (c, 1 - c)]
        lhs = jnp.concatenate([held[pl.ds(pl.multiple_of(s, strip // 2), strip // 2), cut] for s in starts], 0)
        part = lax.dot_general(lhs, held[:, cut], NT, preferred_element_type=f32)
        total = part if total is None else total + part
    off = 0
    for r in range(4):
        for at, ref in ((strip * r, keep_ref), (strip * r + strip // 2, give_ref)):
            ref[:, off:off + per * (r + 1)] = total[at:at + strip // 2, :per * (r + 1)]
        off += per * (r + 1)


def gram(meta, parts, moved):
    per, width = parts[0].shape
    n = 4 * per
    return pl.pallas_call(
        gram_kernel,
        out_shape=[jax.ShapeDtypeStruct((per // 8, 10 * per), f32)] * 2,
        in_specs=[pl.BlockSpec(memory_space=pltpu.SMEM)] + [pl.BlockSpec(memory_space=pl.ANY)] * len(parts) + vmem(1),
        out_specs=vmem(2),
        scratch_shapes=[pltpu.VMEM((n, width), bf16), pltpu.SemaphoreType.DMA((2, len(parts)))],
        compiler_params=pltpu.CompilerParams(vmem_limit_bytes=24 << 20),
        cost_estimate=pl.CostEstimate(flops=2 * per * n * width, bytes_accessed=2 * n * width, transcendentals=0),
    )(meta, *parts, moved)
HI = lax.Precision.HIGHEST
NN = (((1,), (0,)), ((), ()))


def mm(a, b, dims=NN):
    return lax.dot_general(a, b, dims, precision=HI, preferred_element_type=f32)


def factor_tile(tile):
    lane = lax.broadcasted_iota(jnp.int32, (8, 128), 1)
    sub = lax.broadcasted_iota(jnp.int32, (8, 128), 0)
    for p in range(16):
        r0 = 8 * p
        panel = tile[r0:r0 + 8, :]
        inside = (lane >= r0) & (lane < r0 + 8)
        cols = [jnp.broadcast_to(panel[:, r0 + k:r0 + k + 1], (8, 128)) for k in range(8)]
        a = {(i, k): jnp.broadcast_to(cols[k][i:i + 1, :], (8, 128)) for k in range(8) for i in range(k, 8)}
        l = {}
        r = []
        for k in range(8):
            rk = lax.rsqrt(a[k, k])
            r.append(rk)
            for i in range(k + 1, 8):
                l[i, k] = a[i, k] * rk
            for j in range(k + 1, 8):
                for i in range(j, 8):
                    a[i, j] = a[i, j] - l[i, k] * l[j, k]
        eye = jnp.where(lane - r0 == sub, 1.0, 0.0)
        start = jnp.where(inside, eye, panel)
        w = []
        out = jnp.zeros((8, 128), f32)
        for k in range(8):
            x = jnp.broadcast_to(start[k:k + 1, :], (8, 128))
            for m in range(k):
                x = x - l[k, m] * w[m]
            x = x * r[k]
            w.append(x)
            out = jnp.where(sub == k, x, out)
        tile[r0:r0 + 8, :] = out
        if p % 8 + 2 < 8:
            flip = out.T
        for i in range(p + 1, 8 if p < 8 else 16):
            row = tile[8 * i:8 * i + 8, :]
            rest = jnp.where(inside, 0.0, row)
            u = []
            for k in range(8):
                if i > p + DIRECT:
                    u.append(jnp.broadcast_to(flip[8 * i:8 * i + 8, k:k + 1], (8, 128)))
                    continue
                x = jnp.broadcast_to(row[:, r0 + k:r0 + k + 1], (8, 128))
                for m in range(k):
                    x = x - l[k, m] * u[m]
                u.append(x * r[k])
            for k in range(8):
                rest = rest - u[k] * w[k]
            tile[8 * i:8 * i + 8, :] = rest
        if p == 7:
            top = tile[:64, :]
            row = lax.broadcasted_iota(jnp.int32, (64, 128), 0)
            col = lax.broadcasted_iota(jnp.int32, (64, 128), 1)
            done = jnp.where((col <= row) | (col >= 64), top, 0.0)
            tile[64:, :] = jnp.where(col < 64, 0.0, tile[64:, :]) - mm(top[:, 64:], done, TN)


DIRECT = 1


def factor(d, tile, tile2):
    lower = lax.broadcasted_iota(jnp.int32, (128, 128), 1) <= lax.broadcasted_iota(jnp.int32, (128, 128), 0)
    tile[...] = d[:128, :128]
    factor_tile(tile)
    first = jnp.where(lower, tile[...], 0.0)
    up = mm(first, d[:128, 128:])
    tile2[...] = d[128:, 128:] - mm(up, up, TN)
    cross = mm(up, first, TN)
    factor_tile(tile2)
    second = jnp.where(lower, tile2[...], 0.0)
    low = -mm(second, cross)
    return jnp.concatenate([jnp.concatenate([first, jnp.zeros((128, 128), f32)], 1), jnp.concatenate([low, second], 1)], 0)


def stage_kernel(stages, scale, meta_ref, *refs):
    b, c = meta_ref[0], meta_ref[1]
    refs = list(refs)
    last = stages[-1] == 3
    if last:
        held, own, sem = refs.pop(), refs.pop(), refs.pop()
        pieces = [refs.pop(0) for _ in PIECES]
        fresh = refs.pop(0)
        copies = fetches(b, pieces, held, sem)
        for copy in copies:
            copy.start()
    halves = [refs.pop(0), refs.pop(0)]
    lead = {r: refs.pop(0) for r in range(stages[0])}
    for r in stages:
        if not (last and r == stages[-1]):
            lead[r] = refs.pop(0)
    out = refs.pop(0) if last else None
    a_s, tile, tile2 = refs
    off = 0
    for r in stages:
        width = 256 * (r + 1)
        for h in range(2):
            for kb in range(4):
                at = 64 * ((b + kb) % 4) + 32 * (c if h == 0 else 1 - c)
                a_s[pl.ds(pl.multiple_of(at, 32), 32), 0:width] = halves[h][kb, :, off:off + width] * scale
        off += width
        d = a_s[:, 256 * r:width]
        w = []
        for j in range(r):
            w.append(mm(a_s[:, :256 * (j + 1)], lead[j][...], NT))
            d = d - mm(w[j], w[j], NT)
        v = [sum(mm(w[j], lead[j][:, 256 * i:256 * (i + 1)]) for j in range(i, r)) for i in range(r)]
        corner = factor(d, tile, tile2)
        row = jnp.concatenate([-mm(corner, v[i]) for i in range(r)] + [corner], 1) if r else corner
        if last and r == stages[-1]:
            for s in range(4):
                @pl.when(b == s)
                def _():
                    if s == r:
                        own[...] = row.astype(bf16)
                    else:
                        own[:, :256 * (s + 1)] = lead[s][...].astype(bf16)
                        own[:, 256 * (s + 1):] = jnp.zeros((256, 1024 - 256 * (s + 1)), bf16)
        else:
            lead[r][...] = row
    if last:
        for copy in copies:
            copy.wait()
        refresh(b, fresh, held, slice(None), held.shape[1])
        for at in range(0, out.shape[1], 256):
            out[:, at:at + 256] = jnp.dot(own[...], held[:, at:at + 256], preferred_element_type=f32).astype(bf16)


def stage(stages, scale, meta, halves, lead, parts=(), fresh=None):
    last = stages[-1] == 3
    shapes = [jax.ShapeDtypeStruct((256, 256 * (r + 1)), f32) for r in stages[:len(stages) - last]]
    scratch = [pltpu.VMEM((256, 1024), f32), pltpu.VMEM((128, 128), f32), pltpu.VMEM((128, 128), f32)]
    if last:
        shapes.append(jax.ShapeDtypeStruct((256, fresh.shape[1]), bf16))
        scratch += [pltpu.SemaphoreType.DMA((len(parts),)), pltpu.VMEM((256, 1024), bf16), pltpu.VMEM((1024, fresh.shape[1]), bf16)]
    return pl.pallas_call(
        functools.partial(stage_kernel, stages, scale),
        out_shape=shapes,
        in_specs=[pl.BlockSpec(memory_space=pltpu.SMEM)] + [pl.BlockSpec(memory_space=pl.ANY)] * len(parts) + vmem(2 + len(lead) + last),
        out_specs=vmem(len(shapes)),
        scratch_shapes=scratch,
        compiler_params=pltpu.CompilerParams(vmem_limit_bytes=28 << 20),
        cost_estimate=pl.CostEstimate(flops=10 ** 10 * len(stages), bytes_accessed=10 ** 7, transcendentals=0),
    )(meta, *parts, *([fresh] if last else []), *halves, *lead)


def mates(n):
    return [[2 * a + c for a in range(n // 2)] for c in range(2)]


def from_core(v):
    n = lax.axis_size("ga")
    return lax.ppermute(v, "ga", [(g, g ^ 1) for g in range(n)])


def from_band(v, k):
    n = lax.axis_size("band")
    return lax.ppermute(v, "band", [(a, (a - k) % n) for a in range(n)])


def swap_mates(v):
    return lax.all_to_all(v, "ga", split_axis=0, concat_axis=0, tiled=True, axis_index_groups=mates(lax.axis_size("ga")))


def reduce_units(keep, give):
    both = keep + from_core(give)
    return jnp.sum(swap_mates(both.reshape(both.shape[0], 4, -1)), 0)


def spread_units(unit, half):
    return swap_mates(jnp.broadcast_to(unit[None], (half,) + unit.shape))


def spread_bands(rows):
    return jnp.stack([rows] + [from_band(rows, k) for k in range(1, 4)])


def shards(psi, potential, gmap, colxy):
    band_dev, _, gdev = psi.shape
    n_ga = lax.axis_size("ga")
    n_band = lax.axis_size("band")
    points = potential.shape[1]
    scale = 2.0 / (gdev * n_ga)
    cs = tables(points)
    ga_index = lax.axis_index("ga")
    band = lax.axis_index("band")
    c = ga_index % 2
    flat = lax.optimization_barrier(psi.reshape(band_dev, 2 * gdev))
    cross = band_dev // 2
    low, high = flat[:cross], flat[cross:]
    after_low, before_high = from_band(low, 1), from_band(high, -1)
    after_high, before_low = from_band(high, 1), from_band(low, -1)
    psi8 = psi[:FB].reshape(2 * FB, gdev)
    sent = spread(psi8, gmap, cs).reshape(n_ga, 2, 256)
    received = lax.all_to_all(sent, "ga", split_axis=0, concat_axis=0, tiled=True)
    received, after_low, before_high = lax.optimization_barrier((received, after_low, before_high))
    far_low, far_high = from_band(after_low, 1), from_band(before_high, -1)
    val = received.reshape(n_ga, 16, COLS).transpose(1, 0, 2).reshape(16, n_ga * COLS)
    picked = planes(val, colxy, potential, cs)
    picked = picked.reshape(16, n_ga, COLS).transpose(1, 0, 2).reshape(n_ga, 2, 256)
    back = lax.all_to_all(picked, "ga", split_axis=0, concat_axis=0, tiled=True)
    own_columns = lax.dynamic_slice_in_dim(colxy, ga_index * COLS, COLS)
    moved = collect(back.reshape(2 * n_ga, 256), psi8, gmap, own_columns, cs).reshape(FB, 2 * gdev)
    moved, after_high, before_low, far_low, far_high = lax.optimization_barrier((moved, after_high, before_low, far_low, far_high))
    fresh = jnp.stack([moved] + [from_band(moved, k) for k in range(1, n_band)])
    fresh = jnp.pad(fresh, ((0, 0), (0, 16 - FB), (0, 0))).reshape(n_band * 16, 2 * gdev)
    pieces = (flat, after_low, after_high, before_low, before_high, far_low, far_high)
    meta = jnp.stack([band, c]).astype(jnp.int32)
    keep, give = gram(meta, pieces, fresh)
    strip = band_dev // n_band
    rows = spread_units(reduce_units(keep, give), strip // 2).reshape(strip // 2, -1)
    cut = sum(range(1, SPLIT + 1)) * band_dev
    first = spread_bands(rows[:, :cut])
    first, rest = lax.optimization_barrier((first, rows[:, cut:]))
    parts = [from_band(rest, k) for k in range(1, n_band)]
    lead = stage(tuple(range(SPLIT)), scale, meta, (first, from_core(first)), [])
    parts, lead = lax.optimization_barrier((parts, lead))
    second = jnp.stack([rest, *parts])
    rotated = stage(tuple(range(SPLIT, n_band)), scale, meta, (second, from_core(second)), lead, pieces, fresh)[-1]
    return rotated.reshape(band_dev, 2, gdev)


SPLIT = 2


def solution(mesh):
    in_specs = (P("band", None, "ga"), P("ga", None, None), P("ga"), P())
    out_specs = P("band", None, "ga")
    return jax.shard_map(shards, mesh=mesh, in_specs=in_specs, out_specs=out_specs, check_vma=False)
```

```python
import functools
import math

import jax
import jax.numpy as jnp
from jax import lax
from jax.experimental import pallas as pl
from jax.experimental.pallas import tpu as pltpu
from jax.sharding import PartitionSpec as P


COLS = 32
FB = 4
HALF = 40
NT = (((1,), (1,)), ((), ()))
TN = (((0,), (0,)), ((), ()))
f32 = jnp.float32
bf16 = jnp.bfloat16


def tables(points):
    indices = jnp.arange(points, dtype=jnp.int32)
    phase = indices[:, None] * indices[None, :] % points
    angle = phase.astype(f32) * (2.0 * math.pi / points)
    return jnp.concatenate([jnp.cos(angle), jnp.sin(angle)], 0)


def split(x):
    high = x.astype(bf16)
    return high, (x - high.astype(f32)).astype(bf16)


def dot3(a, b, dims=(((1,), (0,)), ((), ()))):
    return lax.dot_general(a, b, dims, precision=lax.Precision.HIGH, preferred_element_type=f32)


def dot1(a, b, dims=(((1,), (0,)), ((), ()))):
    return lax.dot_general(a.astype(bf16), b.astype(bf16), dims, preferred_element_type=f32)


def spread_kernel(psi_ref, gmap_ref, cs_ref, out_ref):
    gdev = psi_ref.shape[1]
    gmap = gmap_ref[...]
    col = gmap // 128
    zpos = gmap % 128
    colmask = lax.broadcasted_iota(jnp.int32, (COLS, gdev), 0) == col
    onez = (lax.broadcasted_iota(jnp.int32, (128, gdev), 0) == zpos).astype(f32).astype(bf16)
    psi = psi_ref[...].astype(f32)
    rows = [jnp.where(colmask, psi[2 * b + ri:2 * b + ri + 1, :], 0.0) for ri in range(2) for b in range(FB)]
    buf = lax.dot_general(jnp.concatenate(rows, 0).astype(bf16), onez, NT, preferred_element_type=f32)
    p = dot3(cs_ref[...], buf, NT)
    re = p[:128, :128] - p[128:, 128:]
    im = p[128:, :128] + p[:128, 128:]
    out_ref[...] = jnp.concatenate([re, im], 1).astype(bf16)


def plane_kernel(rec_ref, colxy_ref, pot_ref, cs_ref, out_ref, g_ref, v_ref, wide, flip):
    senders = rec_ref.shape[0]
    ncols = colxy_ref.shape[1]
    rec = rec_ref[...].astype(f32)
    flip[...] = jnp.concatenate([rec, jnp.zeros((128 - senders, rec.shape[1]), f32)], 0).T
    for t in range(COLS // 2):
        even = flip[pl.ds(2 * t, 16, stride=COLS), :]
        odd = flip[pl.ds(2 * t + 1, 16, stride=COLS), :]
        wide[:, 128 * t:128 * (t + 1)] = even + pltpu.roll(odd, 64, 1)
    place = colxy_ref[...]
    xneg = (128 - place // 128) % 128
    ypos = place % 128
    xmask = lax.broadcasted_iota(jnp.int32, (HALF, ncols), 0) == xneg
    oney = (lax.broadcasted_iota(jnp.int32, (128, ncols), 0) == ypos).astype(f32).astype(bf16)
    items = wide.shape[0]
    for j in range(items):
        a = jnp.where(xmask, wide[j:j + 1, :], 0.0).astype(bf16)
        g_ref[j * HALF:(j + 1) * HALF, :] = lax.dot_general(a, oney, NT, preferred_element_type=f32)
    cs = cs_ref[...]
    p = dot1(g_ref[...], cs, NT)
    xcs = jnp.concatenate([cs[:128, :HALF], cs[128:, :HALF]], 1)
    for zz in range(2):
        for b in range(FB):
            r0 = ((zz * 2) * FB + b) * HALF
            i0 = ((zz * 2 + 1) * FB + b) * HALF
            yr = p[r0:r0 + HALF, :128] - p[i0:i0 + HALF, 128:]
            yi = p[r0:r0 + HALF, 128:] + p[i0:i0 + HALF, :128]
            field = 2.0 * dot1(xcs, jnp.concatenate([yr, yi], 0))
            w = pot_ref[zz] * field
            v = dot1(xcs, w, TN)
            v_ref[r0:r0 + HALF, :] = v[:HALF]
            v_ref[i0:i0 + HALF, :] = v[HALF:]
    q = dot1(v_ref[...], cs, NT)
    for zz in range(2):
        for b in range(FB):
            r0 = ((zz * 2) * FB + b) * HALF
            i0 = ((zz * 2 + 1) * FB + b) * HALF
            re = q[r0:r0 + HALF, :128] + q[i0:i0 + HALF, 128:]
            im = q[i0:i0 + HALF, :128] - q[r0:r0 + HALF, 128:]
            for at, part in ((zz * 2 * FB + b, re), ((zz * 2 + 1) * FB + b, im)):
                t = jnp.dot((part * (2.0 ** -21)).astype(bf16), oney, preferred_element_type=f32)
                wide[at:at + 1, :] = jnp.sum(jnp.where(xmask, t, 0.0), 0, keepdims=True)
    for t in range(COLS // 2):
        pair = wide[:, 128 * t:128 * (t + 1)]
        flip[pl.ds(2 * t, 16, stride=COLS), :] = pair
        flip[pl.ds(2 * t + 1, 16, stride=COLS), :] = pltpu.roll(pair, 64, 1)
    out_ref[...] = flip[...].T[:senders].astype(bf16)


def collect_kernel(back_ref, psi_ref, gmap_ref, colt_ref, cs_ref, out_ref, wide):
    psi = psi_ref[...].astype(f32)
    gdev = psi_ref.shape[1]
    gmap = gmap_ref[...]
    col = gmap // 128
    zpos = gmap % 128
    colmask = lax.broadcasted_iota(jnp.int32, (COLS, gdev), 0) == col
    onez = (lax.broadcasted_iota(jnp.int32, (128, gdev), 0) == zpos).astype(f32).astype(bf16)

    def signed(v):
        return jnp.where(v < 64, v, v - 128).astype(f32)
    place = colt_ref[...]
    sx = signed(place // 128)
    sy = signed(place % 128)
    sz = signed(zpos)
    flat = jnp.sum(jnp.where(colmask, sx * sx + sy * sy, 0.0), 0, keepdims=True)
    kinetic = (flat + sz * sz) * (32.0 / (128 * 128))
    p = dot3(cs_ref[...], back_ref[...].astype(f32))
    re = p[:128, :128] + p[128:, 128:]
    im = p[:128, 128:] - p[128:, :128]
    for ri, spec in ((0, re), (1, im)):
        high, low = split(spec.T)
        t = jnp.dot(high, onez, preferred_element_type=f32) + jnp.dot(low, onez, preferred_element_type=f32)
        for b in range(FB):
            applied = jnp.sum(jnp.where(colmask, t[b * COLS:(b + 1) * COLS, :], 0.0), 0, keepdims=True)
            own = psi[2 * b + ri:2 * b + ri + 1, :]
            hpsi = kinetic * own + applied
            wide[2 * b + ri:2 * b + ri + 1, :] = own - 0.25 * hpsi
    out_ref[...] = wide[...].astype(bf16)


def vmem(n):
    return [pl.BlockSpec(memory_space=pltpu.VMEM)] * n


def call(kernel, shape, n, scratch=()):
    return pl.pallas_call(kernel, out_shape=jax.ShapeDtypeStruct(shape, bf16), in_specs=vmem(n), out_specs=vmem(1)[0],
                          scratch_shapes=list(scratch),
                          compiler_params=pltpu.CompilerParams(vmem_limit_bytes=48 << 20))


def spread(psi8, gmap, cs):
    return call(spread_kernel, (128, 256), 3)(psi8, gmap[None], cs)


def planes(rec, colxy, potential, cs):
    rows = 16 * HALF
    scratch = [pltpu.VMEM((rows, 128), f32)] * 2 + [pltpu.VMEM((16, colxy.shape[0]), f32), pltpu.VMEM((16 * COLS, 128), f32)]
    return call(plane_kernel, rec.shape, 4, scratch)(rec, colxy[None], potential, cs)


def collect(back, psi8, gmap, place, cs):
    return call(collect_kernel, psi8.shape, 5, [pltpu.VMEM(psi8.shape, f32)])(back, psi8, gmap[None], place[:, None], cs)


PIECES = ((0, 0, 2), (1, 0, 1), (1, 1, 1), (3, 0, 1), (3, 1, 1), (2, 0, 1), (2, 1, 1))


def fetches(b, refs, held, sem, cut=slice(None), row=()):
    per = held.shape[0] // 4
    out = []
    for i, (ref, (k, low, n)) in enumerate(zip(refs, PIECES)):
        start = pl.multiple_of((b + k) % 4 * per + low * (per // 2), per // 2)
        out.append(pltpu.make_async_copy(ref.at[:, cut], held.at[pl.ds(start, n * per // 2), cut], sem.at[(*row, i)]))
    return out


def refresh(b, fresh, held, cut, width):
    per = held.shape[0] // 4
    new = lax.broadcasted_iota(jnp.int32, (16, width), 0) < FB
    for k in range(4):
        at = pl.ds(pl.multiple_of((b + k) % 4 * per, per), 16)
        held[at, cut] = jnp.where(new, fresh[16 * k:16 * k + 16, cut].astype(f32), held[at, cut].astype(f32)).astype(bf16)


def gram_kernel(band_ref, *refs):
    pieces = refs[:len(PIECES)]
    fresh, keep_ref, give_ref, held, sem = refs[len(PIECES):]
    b, c = band_ref[0], band_ref[1]
    n, width = held.shape
    per = n // 4
    strip = per // 4
    first = width // 512 * 256
    cuts = ((0, first), (first, width - first))
    copies = [fetches(b, pieces, held, sem, pl.ds(*cut), (h,)) for h, cut in enumerate(cuts)]
    for copy in copies[0] + copies[1]:
        copy.start()
    total = None
    for h, (start, size) in enumerate(cuts):
        for copy in copies[h]:
            copy.wait()
        cut = pl.ds(start, size)
        refresh(b, fresh, held, cut, size)
        starts = [r * per + b * strip + core * (strip // 2) for r in range(4) for core in (c, 1 - c)]
        lhs = jnp.concatenate([held[pl.ds(pl.multiple_of(s, strip // 2), strip // 2), cut] for s in starts], 0)
        part = lax.dot_general(lhs, held[:, cut], NT, preferred_element_type=f32)
        total = part if total is None else total + part
    off = 0
    for r in range(4):
        for at, ref in ((strip * r, keep_ref), (strip * r + strip // 2, give_ref)):
            ref[:, off:off + per * (r + 1)] = total[at:at + strip // 2, :per * (r + 1)]
        off += per * (r + 1)


def gram(meta, parts, moved):
    per, width = parts[0].shape
    n = 4 * per
    return pl.pallas_call(
        gram_kernel,
        out_shape=[jax.ShapeDtypeStruct((per // 8, 10 * per), f32)] * 2,
        in_specs=[pl.BlockSpec(memory_space=pltpu.SMEM)] + [pl.BlockSpec(memory_space=pl.ANY)] * len(parts) + vmem(1),
        out_specs=vmem(2),
        scratch_shapes=[pltpu.VMEM((n, width), bf16), pltpu.SemaphoreType.DMA((2, len(parts)))],
        compiler_params=pltpu.CompilerParams(vmem_limit_bytes=24 << 20),
        cost_estimate=pl.CostEstimate(flops=2 * per * n * width, bytes_accessed=2 * n * width, transcendentals=0),
    )(meta, *parts, moved)
HI = lax.Precision.HIGHEST
NN = (((1,), (0,)), ((), ()))


def mm(a, b, dims=NN):
    return lax.dot_general(a, b, dims, precision=HI, preferred_element_type=f32)


def factor_tile(tile):
    lane = lax.broadcasted_iota(jnp.int32, (8, 128), 1)
    sub = lax.broadcasted_iota(jnp.int32, (8, 128), 0)
    for p in range(16):
        r0 = 8 * p
        panel = tile[r0:r0 + 8, :]
        inside = (lane >= r0) & (lane < r0 + 8)
        cols = [jnp.broadcast_to(panel[:, r0 + k:r0 + k + 1], (8, 128)) for k in range(8)]
        a = {(i, k): jnp.broadcast_to(cols[k][i:i + 1, :], (8, 128)) for k in range(8) for i in range(k, 8)}
        l = {}
        r = []
        for k in range(8):
            rk = lax.rsqrt(a[k, k])
            r.append(rk)
            for i in range(k + 1, 8):
                l[i, k] = a[i, k] * rk
            for j in range(k + 1, 8):
                for i in range(j, 8):
                    a[i, j] = a[i, j] - l[i, k] * l[j, k]
        eye = jnp.where(lane - r0 == sub, 1.0, 0.0)
        start = jnp.where(inside, eye, panel)
        w = []
        out = jnp.zeros((8, 128), f32)
        for k in range(8):
            x = jnp.broadcast_to(start[k:k + 1, :], (8, 128))
            for m in range(k):
                x = x - l[k, m] * w[m]
            x = x * r[k]
            w.append(x)
            out = jnp.where(sub == k, x, out)
        tile[r0:r0 + 8, :] = out
        if p % 8 + 2 < 8:
            flip = out.T
        for i in range(p + 1, 8 if p < 8 else 16):
            row = tile[8 * i:8 * i + 8, :]
            rest = jnp.where(inside, 0.0, row)
            u = []
            for k in range(8):
                if i > p + DIRECT:
                    u.append(jnp.broadcast_to(flip[8 * i:8 * i + 8, k:k + 1], (8, 128)))
                    continue
                x = jnp.broadcast_to(row[:, r0 + k:r0 + k + 1], (8, 128))
                for m in range(k):
                    x = x - l[k, m] * u[m]
                u.append(x * r[k])
            for k in range(8):
                rest = rest - u[k] * w[k]
            tile[8 * i:8 * i + 8, :] = rest
        if p == 7:
            top = tile[:64, :]
            row = lax.broadcasted_iota(jnp.int32, (64, 128), 0)
            col = lax.broadcasted_iota(jnp.int32, (64, 128), 1)
            done = jnp.where((col <= row) | (col >= 64), top, 0.0)
            tile[64:, :] = jnp.where(col < 64, 0.0, tile[64:, :]) - mm(top[:, 64:], done, TN)


DIRECT = 1


def factor(d, tile, tile2):
    lower = lax.broadcasted_iota(jnp.int32, (128, 128), 1) <= lax.broadcasted_iota(jnp.int32, (128, 128), 0)
    tile[...] = d[:128, :128]
    factor_tile(tile)
    first = jnp.where(lower, tile[...], 0.0)
    up = mm(first, d[:128, 128:])
    tile2[...] = d[128:, 128:] - mm(up, up, TN)
    cross = mm(up, first, TN)
    factor_tile(tile2)
    second = jnp.where(lower, tile2[...], 0.0)
    low = -mm(second, cross)
    return jnp.concatenate([jnp.concatenate([first, jnp.zeros((128, 128), f32)], 1), jnp.concatenate([low, second], 1)], 0)


def stage_kernel(stages, scale, meta_ref, *refs):
    b, c = meta_ref[0], meta_ref[1]
    refs = list(refs)
    last = stages[-1] == 3
    if last:
        held, own, sem = refs.pop(), refs.pop(), refs.pop()
        pieces = [refs.pop(0) for _ in PIECES]
        fresh = refs.pop(0)
        copies = fetches(b, pieces, held, sem)
        for copy in copies:
            copy.start()
    halves = [refs.pop(0), refs.pop(0)]
    lead = {r: refs.pop(0) for r in range(stages[0])}
    for r in stages:
        if not (last and r == stages[-1]):
            lead[r] = refs.pop(0)
    out = refs.pop(0) if last else None
    a_s, tile, tile2 = refs
    off = 0
    for r in stages:
        width = 256 * (r + 1)
        for h in range(2):
            for kb in range(4):
                at = 64 * ((b + kb) % 4) + 32 * (c if h == 0 else 1 - c)
                a_s[pl.ds(pl.multiple_of(at, 32), 32), 0:width] = halves[h][kb, :, off:off + width] * scale
        off += width
        d = a_s[:, 256 * r:width]
        w = []
        for j in range(r):
            w.append(mm(a_s[:, :256 * (j + 1)], lead[j][...], NT))
            d = d - mm(w[j], w[j], NT)
        v = [sum(mm(w[j], lead[j][:, 256 * i:256 * (i + 1)]) for j in range(i, r)) for i in range(r)]
        corner = factor(d, tile, tile2)
        row = jnp.concatenate([-mm(corner, v[i]) for i in range(r)] + [corner], 1) if r else corner
        if last and r == stages[-1]:
            for s in range(4):
                @pl.when(b == s)
                def _():
                    if s == r:
                        own[...] = row.astype(bf16)
                    else:
                        own[:, :256 * (s + 1)] = lead[s][...].astype(bf16)
                        own[:, 256 * (s + 1):] = jnp.zeros((256, 1024 - 256 * (s + 1)), bf16)
        else:
            lead[r][...] = row
    if last:
        for copy in copies:
            copy.wait()
        refresh(b, fresh, held, slice(None), held.shape[1])
        for at in range(0, out.shape[1], 256):
            out[:, at:at + 256] = jnp.dot(own[...], held[:, at:at + 256], preferred_element_type=f32).astype(bf16)


def stage(stages, scale, meta, halves, lead, parts=(), fresh=None):
    last = stages[-1] == 3
    shapes = [jax.ShapeDtypeStruct((256, 256 * (r + 1)), f32) for r in stages[:len(stages) - last]]
    scratch = [pltpu.VMEM((256, 1024), f32), pltpu.VMEM((128, 128), f32), pltpu.VMEM((128, 128), f32)]
    if last:
        shapes.append(jax.ShapeDtypeStruct((256, fresh.shape[1]), bf16))
        scratch += [pltpu.SemaphoreType.DMA((len(parts),)), pltpu.VMEM((256, 1024), bf16), pltpu.VMEM((1024, fresh.shape[1]), bf16)]
    return pl.pallas_call(
        functools.partial(stage_kernel, stages, scale),
        out_shape=shapes,
        in_specs=[pl.BlockSpec(memory_space=pltpu.SMEM)] + [pl.BlockSpec(memory_space=pl.ANY)] * len(parts) + vmem(2 + len(lead) + last),
        out_specs=vmem(len(shapes)),
        scratch_shapes=scratch,
        compiler_params=pltpu.CompilerParams(vmem_limit_bytes=28 << 20),
        cost_estimate=pl.CostEstimate(flops=10 ** 10 * len(stages), bytes_accessed=10 ** 7, transcendentals=0),
    )(meta, *parts, *([fresh] if last else []), *halves, *lead)


def mates(n):
    return [[2 * a + c for a in range(n // 2)] for c in range(2)]


def from_core(v):
    n = lax.axis_size("ga")
    return lax.ppermute(v, "ga", [(g, g ^ 1) for g in range(n)])


def from_band(v, k):
    n = lax.axis_size("band")
    return lax.ppermute(v, "band", [(a, (a - k) % n) for a in range(n)])


def swap_mates(v):
    return lax.all_to_all(v, "ga", split_axis=0, concat_axis=0, tiled=True, axis_index_groups=mates(lax.axis_size("ga")))


def reduce_units(keep, give):
    both = keep + from_core(give)
    return jnp.sum(swap_mates(both.reshape(both.shape[0], 4, -1)), 0)


def spread_units(unit, half):
    return swap_mates(jnp.broadcast_to(unit[None], (half,) + unit.shape))


def spread_bands(rows):
    return jnp.stack([rows] + [from_band(rows, k) for k in range(1, 4)])


def shards(psi, potential, gmap, colxy):
    band_dev, _, gdev = psi.shape
    n_ga = lax.axis_size("ga")
    n_band = lax.axis_size("band")
    points = potential.shape[1]
    scale = 2.0 / (gdev * n_ga)
    cs = tables(points)
    ga_index = lax.axis_index("ga")
    band = lax.axis_index("band")
    c = ga_index % 2
    flat = lax.optimization_barrier(psi.reshape(band_dev, 2 * gdev))
    cross = band_dev // 2
    low, high = flat[:cross], flat[cross:]
    after_low, before_high = from_band(low, 1), from_band(high, -1)
    after_high, before_low = from_band(high, 1), from_band(low, -1)
    psi8 = psi[:FB].reshape(2 * FB, gdev)
    sent = spread(psi8, gmap, cs).reshape(n_ga, 2, 256)
    received = lax.all_to_all(sent, "ga", split_axis=0, concat_axis=0, tiled=True)
    received, after_low, before_high = lax.optimization_barrier((received, after_low, before_high))
    far_low, far_high = from_band(after_low, 1), from_band(before_high, -1)
    across = colxy.reshape(n_ga, COLS).T.reshape(-1)
    picked = planes(received.reshape(n_ga, 512), across, potential, cs).reshape(n_ga, 2, 256)
    back = lax.all_to_all(picked, "ga", split_axis=0, concat_axis=0, tiled=True)
    own_columns = lax.dynamic_slice_in_dim(colxy, ga_index * COLS, COLS)
    moved = collect(back.reshape(2 * n_ga, 256), psi8, gmap, own_columns, cs).reshape(FB, 2 * gdev)
    moved, after_high, before_low, far_low, far_high = lax.optimization_barrier((moved, after_high, before_low, far_low, far_high))
    fresh = jnp.stack([moved] + [from_band(moved, k) for k in range(1, n_band)])
    fresh = jnp.pad(fresh, ((0, 0), (0, 16 - FB), (0, 0))).reshape(n_band * 16, 2 * gdev)
    pieces = (flat, after_low, after_high, before_low, before_high, far_low, far_high)
    meta = jnp.stack([band, c]).astype(jnp.int32)
    keep, give = gram(meta, pieces, fresh)
    strip = band_dev // n_band
    rows = spread_units(reduce_units(keep, give), strip // 2).reshape(strip // 2, -1)
    cut = sum(range(1, SPLIT + 1)) * band_dev
    first = spread_bands(rows[:, :cut])
    first, rest = lax.optimization_barrier((first, rows[:, cut:]))
    parts = [from_band(rest, k) for k in range(1, n_band)]
    lead = stage(tuple(range(SPLIT)), scale, meta, (first, from_core(first)), [])
    parts, lead = lax.optimization_barrier((parts, lead))
    second = jnp.stack([rest, *parts])
    rotated = stage(tuple(range(SPLIT, n_band)), scale, meta, (second, from_core(second)), lead, pieces, fresh)[-1]
    return rotated.reshape(band_dev, 2, gdev)


SPLIT = 2


def solution(mesh):
    in_specs = (P("band", None, "ga"), P("ga", None, None), P("ga"), P())
    out_specs = P("band", None, "ga")
    return jax.shard_map(shards, mesh=mesh, in_specs=in_specs, out_specs=out_specs, check_vma=False)
```
